32 devices in a mesh: pair: 2 (over y), rep: 4 (over x, core), blk: 4 (over z).
Axes of the slice: x: 2, y: 2, z: 4, core: 2. Of those that a mesh axis runs over, the one named last changes fastest.
Arguments:
- src_spectra: bfloat16 [64, 8192], P(None, ('pair', 'rep', 'blk')), parts along dimension 1, may hold values from -4 to 4
- tgt_spectra: bfloat16 [64, 8192], P(None, ('pair', 'blk')), parts along dimension 1, may hold values from -4 to 4
- log_src_weight: float32 [8192], P(('pair', 'rep', 'blk')), parts along dimension 0, may hold values from -2 to 2
- log_tgt_weight: float32 [8192], P(('pair', 'blk')), parts along dimension 0, may hold values from -2 to 2
- src_potential: float32 [8192], P(('pair', 'rep', 'blk')), parts along dimension 0, may hold values from -4 to 250
- tgt_potential: float32 [8192], P(('pair', 'blk')), parts along dimension 0, may hold values from -4 to 250
Outputs:
- src_updated: float32 [8192], P(('pair', 'rep', 'blk')), parts along dimension 0
- tgt_updated: float32 [8192], P(('pair', 'blk')), parts along dimension 0
The draws below stay inside these ranges and needn't reach their ends.
There are 2 independent parts, one for each index of `pair`. The reference program is written for one: setup_inputs(seed, part) draws one part's arguments, and reference() takes and returns one part's arrays. A program takes and returns all parts, laid end to end along the dimension named above; each array names one. Nothing has to cross between parts.
All inputs are finite; a program needn't handle non-finite values.
Results may differ from the reference program's by a relative error of at most 0.0003.
Values may be sent and summed in bfloat16 or wider, within the bound.
A program may use at most 128 MiB of HBM per device.

```python
import jax
import jax.numpy as jnp
from jax import lax

C = 64
PIXELS = 4096


def spectra(key, salt):
    base = jax.random.fold_in(key, salt)
    values = jnp.clip(0.35 * jax.random.normal(base, (C, PIXELS), jnp.float32), -4.0, 4.0)
    return values


def potential(key, salt):
    base = jax.random.fold_in(key, salt)
    values = jnp.clip(jax.random.normal(base, (PIXELS,), jnp.float32), -4.0, 4.0)
    return values


def draw_src_spectra(key, part):
    return spectra(key, 11).astype(jnp.bfloat16)


def draw_tgt_spectra(key, part):
    return spectra(key, 23).astype(jnp.bfloat16)


def draw_src_potential(key, part):
    return potential(key, 37)


def draw_tgt_potential(key, part):
    return potential(key, 41)


def shard_levels(stream_key, shape, shards, smallest, largest):
    def one(axis_at, shards_of):
        draws = jax.random.uniform(jax.random.fold_in(jax.random.fold_in(stream_key, 6), axis_at), (shards_of,), jnp.float32, smallest / len(shards), largest / len(shards))
        return jnp.repeat(jnp.exp(draws), shape[axis_at] // shards_of).reshape((-1,) + (1,) * (len(shape) - axis_at - 1))

    factor_of = one(*shards[0])
    for cut in shards[1:]:
        factor_of = factor_of * one(*cut)
    return factor_of


def setup_inputs(seed: int = 0, part: int = 0) -> dict:
    streams_of = jax.random.split(jax.random.key(seed), 7)
    part_splits = jax.random.split(jax.random.fold_in(streams_of[6], part), 7)
    return {
        "src_spectra": draw_src_spectra(jax.random.fold_in(jax.random.fold_in(streams_of[6], part), 71), part),
        "tgt_spectra": draw_tgt_spectra(jax.random.fold_in(jax.random.fold_in(streams_of[6], part), 71), part),
        "log_src_weight": jnp.clip(jax.random.uniform(part_splits[2], (PIXELS,), jnp.float32, -2.0, 2.0) * shard_levels(part_splits[2], (PIXELS,), ((0, 16),), -0.4, 0.0), -2.0, 2.0),
        "log_tgt_weight": jnp.clip(jax.random.uniform(part_splits[3], (PIXELS,), jnp.float32, -2.0, 2.0) * shard_levels(part_splits[3], (PIXELS,), ((0, 4),), -0.4, 0.0), -2.0, 2.0),
        "src_potential": draw_src_potential(jax.random.fold_in(jax.random.fold_in(streams_of[6], part), 71), part),
        "tgt_potential": draw_tgt_potential(jax.random.fold_in(jax.random.fold_in(streams_of[6], part), 71), part),
    }


def reference(src_spectra, tgt_spectra, log_src_weight, log_tgt_weight, src_potential, tgt_potential):
    src_float = src_spectra.astype(jnp.float32)
    tgt_float = tgt_spectra.astype(jnp.float32)
    src_square = 0.5 * jnp.sum(src_float * src_float, axis=0)
    tgt_square = 0.5 * jnp.sum(tgt_float * tgt_float, axis=0)
    src_bias = log_src_weight + src_potential
    tgt_bias = log_tgt_weight + tgt_potential
    count = src_spectra.shape[1]
    rows_block = 512 if count % 512 == 0 else count
    blocks = count // rows_block

    def absorb(carry, block_index):
        col_peak, col_totals = carry
        offset = (block_index * rows_block).astype(jnp.int32)
        block = lax.dynamic_slice_in_dim(src_spectra, offset, rows_block, 1)
        square = lax.dynamic_slice_in_dim(src_square, offset, rows_block, 0)
        bias = lax.dynamic_slice_in_dim(src_bias, offset, rows_block, 0)
        products = lax.dot_general(block, tgt_spectra, (((0,), (0,)), ((), ())), preferred_element_type=jnp.float32)
        cost_tile = square[:, None] + tgt_square[None, :] - products
        row_scores = tgt_bias[None, :] - cost_tile
        row_peak = jnp.max(row_scores, axis=1)
        src_new = -(row_peak + jnp.log(jnp.sum(jnp.exp(row_scores - row_peak[:, None]), axis=1)))
        col_scores = bias[:, None] - cost_tile
        block_peak = jnp.max(col_scores, axis=0)
        block_totals = jnp.sum(jnp.exp(col_scores - block_peak[None, :]), axis=0)
        joined = jnp.maximum(col_peak, block_peak)
        col_totals = col_totals * jnp.exp(col_peak - joined) + block_totals * jnp.exp(block_peak - joined)
        return (joined, col_totals), src_new

    start_peak = jnp.full((count,), -jnp.inf, jnp.float32)
    start_totals = jnp.zeros((count,), jnp.float32)
    (col_peak, col_totals), src_blocks = lax.scan(absorb, (start_peak, start_totals), jnp.arange(blocks, dtype=jnp.int32))
    src_new = src_blocks.reshape(-1)
    tgt_new = -(col_peak + jnp.log(col_totals))
    return 0.5 * (src_potential + src_new), 0.5 * (tgt_potential + tgt_new)
```

```python
import functools

import jax
import jax.numpy as jnp
from jax import lax
from jax.experimental import pallas as pl
from jax.experimental.pallas import tpu as pltpu
from jax.sharding import PartitionSpec as P

MESH = pl.DeviceIdType.MESH
SUBLANES = 8
EXTRA = 16
TILE = 256


def nearest(me, count, k):
    short = jnp.minimum(me, count - 1 - me)
    step = (k + 1) // 2
    both = me + jnp.where(k % 2 == 1, step, -step)
    both = jnp.where(me * 2 < count, both, 2 * me - both)
    far = jnp.where(me * 2 < count, k, count - 1 - k)
    return jnp.where(k <= 2 * short, both, far)


def in_three(value):
    high = value.astype(jnp.bfloat16).astype(jnp.float32)
    middle = (value - high).astype(jnp.bfloat16).astype(jnp.float32)
    return high, middle, value - high - middle


def bias_rows(value, first):
    high, middle, low = in_three(value)
    row = lax.broadcasted_iota(jnp.int32, (EXTRA, value.shape[1]), 0)
    out = jnp.where(row < 6, 1.0, 0.0)
    out = jnp.where(row == first, high, out)
    out = jnp.where(row == first + 1, middle, out)
    out = jnp.where(row == first + 2, low, out)
    return out.astype(jnp.bfloat16)


def half_square(block):
    wide = block.astype(jnp.float32)
    return 0.5 * jnp.sum(wide * wide, axis=0, keepdims=True)


def peak_and_sum(scores):
    rows, width = scores.shape
    grouped = scores.reshape(rows // SUBLANES, SUBLANES, width)
    peak = jnp.max(grouped, axis=0)
    return peak, jnp.sum(jnp.exp(grouped - peak[None]), axis=0)


def joined(earlier, later):
    peak = jnp.maximum(earlier[0], later[0])
    return peak, earlier[1] * jnp.exp(earlier[0] - peak) + later[1] * jnp.exp(later[0] - peak)


def folded(peak, total):
    top = jnp.max(peak, axis=0, keepdims=True)
    return top, jnp.sum(total * jnp.exp(peak - top), axis=0, keepdims=True)


def kernel(
    blocks, copies,
    src_hbm, tgt_hbm, lsw_hbm, ltw_hbm, sp_hbm, tp_hbm,
    src_out, tgt_out,
    slots, biases, tgt_v, lsw, ltw, sp, tp, tgt_flat, tgt_tall, row_mine, row_stats, col_peak, col_total,
    col_stats,
    load_sem, slot_send, slot_recv, bias_send, bias_recv, row_send, row_recv, col_send, col_recv,
):
    me = lax.axis_index("blk")
    rep = lax.axis_index("rep")
    bands, width = src_hbm.shape
    tgt_width = tgt_hbm.shape[1]

    barrier = pltpu.get_barrier_semaphore()
    for k in range(1, blocks):
        pl.semaphore_signal(
            barrier, inc=1, device_id={"blk": (me + k) % blocks}, device_id_type=MESH
        )
    for k in range(1, copies):
        pl.semaphore_signal(
            barrier, inc=1, device_id={"rep": (rep + k) % copies}, device_id_type=MESH
        )
    loads = [
        pltpu.make_async_copy(src_hbm, slots.at[me], load_sem.at[0]),
        pltpu.make_async_copy(lsw_hbm, lsw, load_sem.at[1]),
        pltpu.make_async_copy(sp_hbm, sp, load_sem.at[2]),
        pltpu.make_async_copy(tgt_hbm, tgt_v, load_sem.at[3]),
        pltpu.make_async_copy(ltw_hbm, ltw, load_sem.at[4]),
        pltpu.make_async_copy(tp_hbm, tp, load_sem.at[5]),
    ]
    for load in loads:
        load.start()
    pl.semaphore_wait(barrier, blocks + copies - 2)

    def slot_copy(place, peer):
        return pltpu.make_async_remote_copy(
            src_ref=src_hbm, dst_ref=slots.at[place],
            send_sem=slot_send.at[peer], recv_sem=slot_recv.at[place],
            device_id={"blk": peer}, device_id_type=MESH,
        )

    def bias_copy(place, peer):
        return pltpu.make_async_remote_copy(
            src_ref=biases.at[me], dst_ref=biases.at[place],
            send_sem=bias_send.at[peer], recv_sem=bias_recv.at[place],
            device_id={"blk": peer}, device_id_type=MESH,
        )

    def row_copy(place, peer):
        return pltpu.make_async_remote_copy(
            src_ref=row_mine.at[peer], dst_ref=row_stats.at[place],
            send_sem=row_send.at[peer], recv_sem=row_recv.at[place],
            device_id={"blk": peer}, device_id_type=MESH,
        )

    def col_copy(place, peer):
        return pltpu.make_async_remote_copy(
            src_ref=col_stats.at[rep], dst_ref=col_stats.at[place],
            send_sem=col_send.at[peer], recv_sem=col_recv.at[place],
            device_id={"rep": peer}, device_id_type=MESH,
        )

    for k in range(1, blocks):
        slot_copy(me, nearest(me, blocks, k)).start()
    for load in loads[:3]:
        load.wait()
    src_bias = lsw[...] + sp[...]
    biases[me] = src_bias - half_square(slots[me])
    for k in range(1, blocks):
        bias_copy(me, nearest(me, blocks, k)).start()
    for load in loads[3:]:
        load.wait()
    tgt_bias = ltw[...] + tp[...]
    tgt_flat[pl.ds(0, bands), :] = tgt_v[...]
    tgt_flat[pl.ds(bands, EXTRA), :] = bias_rows(tgt_bias - half_square(tgt_v[...]), 3)
    for at in range(0, tgt_width, TILE):
        tgt_tall[pl.ds(at, TILE), :] = tgt_flat[:, pl.ds(at, TILE)].T
    col_peak[...] = jnp.full_like(col_peak, -jnp.inf)
    col_total[...] = jnp.zeros_like(col_total)

    def turn(k, carry):
        place = nearest(me, blocks, k)

        @pl.when(k > 0)
        def _():
            slot_copy(place, place).wait_recv()
            bias_copy(place, place).wait_recv()

        src = jnp.concatenate([slots[place], bias_rows(biases[place], 0)], axis=0)
        src_tall = src.T
        row = None
        for at in range(0, tgt_width, TILE):
            across = jnp.dot(
                tgt_tall[pl.ds(at, TILE), :], src, preferred_element_type=jnp.float32
            )
            part = peak_and_sum(across)
            row = part if row is None else joined(row, part)
            down = jnp.dot(
                src_tall, tgt_flat[:, pl.ds(at, TILE)], preferred_element_type=jnp.float32
            )
            here = (slice(None), pl.ds(at, TILE))
            col_peak[here], col_total[here] = joined(
                (col_peak[here], col_total[here]), peak_and_sum(down)
            )
        top, total = folded(*row)
        stats = jnp.concatenate([top, total], axis=0)

        @pl.when(k > 0)
        def _():
            row_mine[place] = stats
            row_copy(me, place).start()

        @pl.when(k == 0)
        def _():
            row_stats[me] = stats

        return carry

    lax.fori_loop(0, blocks, turn, 0)
    top, total = folded(col_peak[...], col_total[...])
    col_stats[rep] = jnp.concatenate([top, total], axis=0)
    for k in range(1, copies):
        col_copy(rep, (rep + k) % copies).start()

    for k in range(1, blocks):
        place = nearest(me, blocks, k)
        row_copy(place, place).wait_recv()
    every = row_stats[...]
    top = jnp.max(every[:, 0, :], axis=0, keepdims=True)
    total = jnp.sum(every[:, 1, :] * jnp.exp(every[:, 0, :] - top), axis=0, keepdims=True)
    src_out[...] = 0.5 * (sp[...] + (src_bias - (top + jnp.log(total))))

    for k in range(1, copies):
        place = (rep + k) % copies
        col_copy(place, place).wait_recv()
    every = col_stats[...]
    top = jnp.max(every[:, 0, :], axis=0, keepdims=True)
    total = jnp.sum(every[:, 1, :] * jnp.exp(every[:, 0, :] - top), axis=0, keepdims=True)
    tgt_out[...] = 0.5 * (tp[...] + (tgt_bias - (top + jnp.log(total))))

    for k in range(1, blocks):
        peer = nearest(me, blocks, k)
        slot_copy(me, peer).wait_send()
        bias_copy(me, peer).wait_send()
        row_copy(me, peer).wait_send()
    for k in range(1, copies):
        col_copy(rep, (rep + k) % copies).wait_send()


def on_device(
    blocks, copies,
    src_spectra, tgt_spectra, log_src_weight, log_tgt_weight, src_potential, tgt_potential,
):
    bands, width = src_spectra.shape
    tgt_width = tgt_spectra.shape[1]
    depth = bands + EXTRA
    one = lambda vector: vector.reshape(1, -1)
    f32, bf16 = jnp.float32, jnp.bfloat16
    dma = pltpu.SemaphoreType.DMA
    elements = blocks * width * tgt_width
    src_updated, tgt_updated = pl.pallas_call(
        functools.partial(kernel, blocks, copies),
        out_shape=(
            jax.ShapeDtypeStruct((1, width), f32),
            jax.ShapeDtypeStruct((1, tgt_width), f32),
        ),
        in_specs=[pl.BlockSpec(memory_space=pl.ANY)] * 6,
        out_specs=(pl.BlockSpec(memory_space=pltpu.VMEM), pl.BlockSpec(memory_space=pltpu.VMEM)),
        scratch_shapes=[
            pltpu.VMEM((blocks, bands, width), bf16),
            pltpu.VMEM((blocks, 1, width), f32),
            pltpu.VMEM((bands, tgt_width), bf16),
            pltpu.VMEM((1, width), f32),
            pltpu.VMEM((1, tgt_width), f32),
            pltpu.VMEM((1, width), f32),
            pltpu.VMEM((1, tgt_width), f32),
            pltpu.VMEM((depth, tgt_width), bf16),
            pltpu.VMEM((tgt_width, depth), bf16),
            pltpu.VMEM((blocks, 2, width), f32),
            pltpu.VMEM((blocks, 2, width), f32),
            pltpu.VMEM((SUBLANES, tgt_width), f32),
            pltpu.VMEM((SUBLANES, tgt_width), f32),
            pltpu.VMEM((copies, 2, tgt_width), f32),
            dma((6,)),
            dma((blocks,)), dma((blocks,)),
            dma((blocks,)), dma((blocks,)),
            dma((blocks,)), dma((blocks,)),
            dma((copies,)), dma((copies,)),
        ],
        compiler_params=pltpu.CompilerParams(
            collective_id=0, has_side_effects=True, vmem_limit_bytes=32 * 1024 * 1024
        ),
        cost_estimate=pl.CostEstimate(
            flops=4 * elements * bands, bytes_accessed=4 * bands * tgt_width, transcendentals=2 * elements
        ),
        name="sinkhorn",
    )(
        src_spectra, tgt_spectra, one(log_src_weight), one(log_tgt_weight),
        one(src_potential), one(tgt_potential),
    )
    return src_updated.reshape(-1), tgt_updated.reshape(-1)


def solution(mesh):
    placed = (
        P(None, ("pair", "rep", "blk")),
        P(None, ("pair", "blk")),
        P(("pair", "rep", "blk")),
        P(("pair", "blk")),
        P(("pair", "rep", "blk")),
        P(("pair", "blk")),
    )
    return jax.shard_map(
        functools.partial(on_device, mesh.shape["blk"], mesh.shape["rep"]),
        mesh=mesh,
        in_specs=placed,
        out_specs=(P(("pair", "rep", "blk")), P(("pair", "blk"))),
        check_vma=False,
    )
```

```python
import functools

import jax
import jax.numpy as jnp
from jax import lax
from jax.experimental import pallas as pl
from jax.experimental.pallas import tpu as pltpu
from jax.sharding import PartitionSpec as P

MESH = pl.DeviceIdType.MESH
SUBLANES = 8
EXTRA = 16
DEPTH = 128
TILE = 256


def nearest(me, count, k):
    short = jnp.minimum(me, count - 1 - me)
    step = (k + 1) // 2
    both = me + jnp.where(k % 2 == 1, step, -step)
    both = jnp.where(me * 2 < count, both, 2 * me - both)
    far = jnp.where(me * 2 < count, k, count - 1 - k)
    return jnp.where(k <= 2 * short, both, far)


def in_three(value):
    high = value.astype(jnp.bfloat16).astype(jnp.float32)
    middle = (value - high).astype(jnp.bfloat16).astype(jnp.float32)
    return high, middle, value - high - middle


def bias_rows(value, first):
    high, middle, low = in_three(value)
    row = lax.broadcasted_iota(jnp.int32, (EXTRA, value.shape[1]), 0)
    out = jnp.where(row < 6, 1.0, 0.0)
    out = jnp.where(row == first, high, out)
    out = jnp.where(row == first + 1, middle, out)
    out = jnp.where(row == first + 2, low, out)
    return out.astype(jnp.bfloat16)


def half_square(block):
    wide = block.astype(jnp.float32)
    return 0.5 * jnp.sum(wide * wide, axis=0, keepdims=True)


def by_sublane(scores):
    rows, width = scores.shape
    return scores.reshape(rows // SUBLANES, SUBLANES, width)


def joined(earlier, later):
    peak = jnp.maximum(earlier[0], later[0])
    return peak, earlier[1] * jnp.exp(earlier[0] - peak) + later[1] * jnp.exp(later[0] - peak)


def folded(peak, total):
    top = jnp.max(peak, axis=0, keepdims=True)
    return top, jnp.sum(total * jnp.exp(peak - top), axis=0, keepdims=True)


def kernel(
    blocks, copies,
    src_hbm, tgt_hbm, lsw_hbm, ltw_hbm, sp_hbm, tp_hbm,
    src_out, tgt_out,
    slots, biases, tgt_v, lsw, ltw, sp, tp, tgt_flat, tgt_tall, scores, row_mine, row_stats, col_peak, col_total,
    col_stats,
    load_sem, slot_send, slot_recv, bias_send, bias_recv, row_send, row_recv, col_send, col_recv,
):
    me = lax.axis_index("blk")
    rep = lax.axis_index("rep")
    bands, width = src_hbm.shape
    tgt_width = tgt_hbm.shape[1]
    depth = tgt_flat.shape[0]

    barrier = pltpu.get_barrier_semaphore()
    for k in range(1, blocks):
        pl.semaphore_signal(
            barrier, inc=1, device_id={"blk": (me + k) % blocks}, device_id_type=MESH
        )
    for k in range(1, copies):
        pl.semaphore_signal(
            barrier, inc=1, device_id={"rep": (rep + k) % copies}, device_id_type=MESH
        )
    loads = [
        pltpu.make_async_copy(src_hbm, slots.at[me], load_sem.at[0]),
        pltpu.make_async_copy(lsw_hbm, lsw, load_sem.at[1]),
        pltpu.make_async_copy(sp_hbm, sp, load_sem.at[2]),
        pltpu.make_async_copy(tgt_hbm, tgt_v, load_sem.at[3]),
        pltpu.make_async_copy(ltw_hbm, ltw, load_sem.at[4]),
        pltpu.make_async_copy(tp_hbm, tp, load_sem.at[5]),
    ]
    for load in loads:
        load.start()
    pl.semaphore_wait(barrier, blocks + copies - 2)

    def slot_copy(place, peer):
        return pltpu.make_async_remote_copy(
            src_ref=src_hbm, dst_ref=slots.at[place],
            send_sem=slot_send.at[peer], recv_sem=slot_recv.at[place],
            device_id={"blk": peer}, device_id_type=MESH,
        )

    def bias_copy(place, peer):
        return pltpu.make_async_remote_copy(
            src_ref=biases.at[me], dst_ref=biases.at[place],
            send_sem=bias_send.at[peer], recv_sem=bias_recv.at[place],
            device_id={"blk": peer}, device_id_type=MESH,
        )

    def row_copy(place, peer):
        return pltpu.make_async_remote_copy(
            src_ref=row_mine.at[peer], dst_ref=row_stats.at[place],
            send_sem=row_send.at[peer], recv_sem=row_recv.at[place],
            device_id={"blk": peer}, device_id_type=MESH,
        )

    def col_copy(place, peer):
        return pltpu.make_async_remote_copy(
            src_ref=col_stats.at[rep], dst_ref=col_stats.at[place],
            send_sem=col_send.at[peer], recv_sem=col_recv.at[place],
            device_id={"rep": peer}, device_id_type=MESH,
        )

    for k in range(1, blocks):
        slot_copy(me, nearest(me, blocks, k)).start()
    for load in loads[:3]:
        load.wait()
    src_bias = lsw[...] + sp[...]
    biases[me] = src_bias - half_square(slots[me])
    for k in range(1, blocks):
        bias_copy(me, nearest(me, blocks, k)).start()
    for load in loads[3:]:
        load.wait()
    tgt_bias = ltw[...] + tp[...]
    tgt_flat[pl.ds(0, bands), :] = tgt_v[...]
    if depth > bands + EXTRA:
        tgt_flat[pl.ds(bands + EXTRA, depth - bands - EXTRA), :] = jnp.zeros(
            (depth - bands - EXTRA, tgt_width), jnp.bfloat16
        )
    tgt_flat[pl.ds(bands, EXTRA), :] = bias_rows(tgt_bias - half_square(tgt_v[...]), 3)
    for at in range(0, tgt_width, TILE):
        tgt_tall[pl.ds(at, TILE), :] = tgt_flat[:, pl.ds(at, TILE)].T
    col_peak[...] = jnp.full_like(col_peak, -jnp.inf)
    col_total[...] = jnp.zeros_like(col_total)

    def turn(k, carry):
        place = nearest(me, blocks, k)

        @pl.when(k > 0)
        def _():
            slot_copy(place, place).wait_recv()
            bias_copy(place, place).wait_recv()

        src = [slots[place], bias_rows(biases[place], 0)]
        if depth > bands + EXTRA:
            src.append(jnp.zeros((depth - bands - EXTRA, width), jnp.bfloat16))
        src = jnp.concatenate(src, axis=0)
        src_tall = src.T
        parts = []

        def finish(peak, slot, at, down):
            total = jnp.sum(jnp.exp(by_sublane(scores[slot]) - peak[None]), axis=0)
            if down:
                here = (slice(None), pl.ds(at, TILE))
                col_peak[here], col_total[here] = joined(
                    (col_peak[here], col_total[here]), (peak, total)
                )
            else:
                parts.append((peak, total))

        waiting = None
        for at in range(0, tgt_width, TILE):
            for down in (False, True):
                if down:
                    block = jnp.dot(
                        src_tall, tgt_flat[:, pl.ds(at, TILE)], preferred_element_type=jnp.float32
                    )
                else:
                    block = jnp.dot(
                        tgt_tall[pl.ds(at, TILE), :], src, preferred_element_type=jnp.float32
                    )
                slot = 2 * (at // TILE) + down
                scores[slot] = block
                peak = jnp.max(by_sublane(block), axis=0)
                if waiting is not None:
                    finish(*waiting)
                waiting = (peak, slot, at, down)
        finish(*waiting)
        top, total = folded(*functools.reduce(joined, parts))
        stats = jnp.concatenate([top, total], axis=0)

        @pl.when(k > 0)
        def _():
            row_mine[place] = stats
            row_copy(me, place).start()

        @pl.when(k == 0)
        def _():
            row_stats[me] = stats

        return carry

    lax.fori_loop(0, blocks, turn, 0)
    top, total = folded(col_peak[...], col_total[...])
    col_stats[rep] = jnp.concatenate([top, total], axis=0)
    for k in range(1, copies):
        col_copy(rep, (rep + k) % copies).start()

    for k in range(1, blocks):
        place = nearest(me, blocks, k)
        row_copy(place, place).wait_recv()
    every = row_stats[...]
    top = jnp.max(every[:, 0, :], axis=0, keepdims=True)
    total = jnp.sum(every[:, 1, :] * jnp.exp(every[:, 0, :] - top), axis=0, keepdims=True)
    src_out[...] = 0.5 * (sp[...] + (src_bias - (top + jnp.log(total))))

    for k in range(1, copies):
        place = (rep + k) % copies
        col_copy(place, place).wait_recv()
    every = col_stats[...]
    top = jnp.max(every[:, 0, :], axis=0, keepdims=True)
    total = jnp.sum(every[:, 1, :] * jnp.exp(every[:, 0, :] - top), axis=0, keepdims=True)
    tgt_out[...] = 0.5 * (tp[...] + (tgt_bias - (top + jnp.log(total))))

    for k in range(1, blocks):
        peer = nearest(me, blocks, k)
        slot_copy(me, peer).wait_send()
        bias_copy(me, peer).wait_send()
        row_copy(me, peer).wait_send()
    for k in range(1, copies):
        col_copy(rep, (rep + k) % copies).wait_send()


def write_out(src, tgt, src_out, tgt_out, sem):
    copies = [
        pltpu.make_async_copy(src, src_out, sem.at[0]),
        pltpu.make_async_copy(tgt, tgt_out, sem.at[1]),
    ]
    for copy in copies:
        copy.start()
    for copy in copies:
        copy.wait()


def on_device(
    blocks, copies,
    src_spectra, tgt_spectra, log_src_weight, log_tgt_weight, src_potential, tgt_potential,
):
    bands, width = src_spectra.shape
    tgt_width = tgt_spectra.shape[1]
    depth = -(-(bands + EXTRA) // DEPTH) * DEPTH
    one = lambda vector: vector.reshape(1, -1)
    f32, bf16 = jnp.float32, jnp.bfloat16
    dma = pltpu.SemaphoreType.DMA
    elements = blocks * width * tgt_width
    src_updated, tgt_updated = pl.pallas_call(
        functools.partial(kernel, blocks, copies),
        out_shape=(pltpu.VMEM((1, width), f32), pltpu.VMEM((1, tgt_width), f32)),
        in_specs=[pl.BlockSpec(memory_space=pltpu.HBM)] * 6,
        out_specs=(pl.BlockSpec(memory_space=pltpu.VMEM), pl.BlockSpec(memory_space=pltpu.VMEM)),
        scratch_shapes=[
            pltpu.VMEM((blocks, bands, width), bf16),
            pltpu.VMEM((blocks, 1, width), f32),
            pltpu.VMEM((bands, tgt_width), bf16),
            pltpu.VMEM((1, width), f32),
            pltpu.VMEM((1, tgt_width), f32),
            pltpu.VMEM((1, width), f32),
            pltpu.VMEM((1, tgt_width), f32),
            pltpu.VMEM((depth, tgt_width), bf16),
            pltpu.VMEM((tgt_width, depth), bf16),
            pltpu.VMEM((2 * tgt_width // TILE, TILE, TILE), f32),
            pltpu.VMEM((blocks, 2, width), f32),
            pltpu.VMEM((blocks, 2, width), f32),
            pltpu.VMEM((SUBLANES, tgt_width), f32),
            pltpu.VMEM((SUBLANES, tgt_width), f32),
            pltpu.VMEM((copies, 2, tgt_width), f32),
            dma((6,)),
            dma((blocks,)), dma((blocks,)),
            dma((blocks,)), dma((blocks,)),
            dma((blocks,)), dma((blocks,)),
            dma((copies,)), dma((copies,)),
        ],
        compiler_params=pltpu.CompilerParams(
            collective_id=0, has_side_effects=True, vmem_limit_bytes=32 * 1024 * 1024
        ),
        cost_estimate=pl.CostEstimate(
            flops=4 * elements * bands, bytes_accessed=4 * bands * tgt_width, transcendentals=2 * elements
        ),
        name="sinkhorn",
    )(
        *(
            pltpu.with_memory_space_constraint(array, pltpu.HBM)
            for array in (
                src_spectra, tgt_spectra, one(log_src_weight), one(log_tgt_weight),
                one(src_potential), one(tgt_potential),
            )
        )
    )
    src_updated, tgt_updated = pl.pallas_call(
        write_out,
        out_shape=(
            jax.ShapeDtypeStruct((1, width), f32),
            jax.ShapeDtypeStruct((1, tgt_width), f32),
        ),
        in_specs=[pl.BlockSpec(memory_space=pltpu.VMEM)] * 2,
        out_specs=(pl.BlockSpec(memory_space=pltpu.HBM), pl.BlockSpec(memory_space=pltpu.HBM)),
        scratch_shapes=[dma((2,))],
        name="write_out",
    )(src_updated, tgt_updated)
    return src_updated.reshape(-1), tgt_updated.reshape(-1)


def solution(mesh):
    placed = (
        P(None, ("pair", "rep", "blk")),
        P(None, ("pair", "blk")),
        P(("pair", "rep", "blk")),
        P(("pair", "blk")),
        P(("pair", "rep", "blk")),
        P(("pair", "blk")),
    )
    return jax.shard_map(
        functools.partial(on_device, mesh.shape["blk"], mesh.shape["rep"]),
        mesh=mesh,
        in_specs=placed,
        out_specs=(P(("pair", "rep", "blk")), P(("pair", "blk"))),
        check_vma=False,
    )
```

```python
import functools

import jax
import jax.numpy as jnp
from jax import lax
from jax.experimental import pallas as pl
from jax.experimental.pallas import tpu as pltpu
from jax.sharding import PartitionSpec as P

MESH = pl.DeviceIdType.MESH
SUBLANES = 8
WIDE = 32
EXTRA = 16
DEPTH = 128
TILE = 256


def nearest(me, count, k):
    short = jnp.minimum(me, count - 1 - me)
    step = (k + 1) // 2
    both = me + jnp.where(k % 2 == 1, step, -step)
    both = jnp.where(me * 2 < count, both, 2 * me - both)
    far = jnp.where(me * 2 < count, k, count - 1 - k)
    return jnp.where(k <= 2 * short, both, far)


def in_three(value):
    high = value.astype(jnp.bfloat16).astype(jnp.float32)
    middle = (value - high).astype(jnp.bfloat16).astype(jnp.float32)
    return high, middle, value - high - middle


def bias_rows(value, first):
    high, middle, low = in_three(value)
    row = lax.broadcasted_iota(jnp.int32, (EXTRA, value.shape[1]), 0)
    out = jnp.where(row < 6, 1.0, 0.0)
    out = jnp.where(row == first, high, out)
    out = jnp.where(row == first + 1, middle, out)
    out = jnp.where(row == first + 2, low, out)
    return out.astype(jnp.bfloat16)


def half_square(block):
    wide = block.astype(jnp.float32)
    return 0.5 * jnp.sum(wide * wide, axis=0, keepdims=True)


def grouped(scores, group):
    rows, width = scores.shape
    return scores.reshape(rows // group, group, width)


def joined(earlier, later):
    peak = jnp.maximum(earlier[0], later[0])
    return peak, earlier[1] * jnp.exp(earlier[0] - peak) + later[1] * jnp.exp(later[0] - peak)


def folded(peak, total):
    top = jnp.max(peak, axis=0, keepdims=True)
    return top, jnp.sum(total * jnp.exp(peak - top), axis=0, keepdims=True)


def kernel(
    blocks, copies,
    src_hbm, tgt_hbm, lsw_hbm, ltw_hbm, sp_hbm, tp_hbm,
    src_out, tgt_out,
    slots, biases, tgt_v, lsw, ltw, sp, tp, tgt_flat, tgt_tall, across, down, row_mine, row_stats, col_peak, col_total,
    col_stats,
    load_sem, slot_send, slot_recv, bias_send, bias_recv, row_send, row_recv, col_send, col_recv,
):
    me = lax.axis_index("blk")
    rep = lax.axis_index("rep")
    bands, width = src_hbm.shape
    tgt_width = tgt_hbm.shape[1]
    depth = tgt_flat.shape[0]

    barrier = pltpu.get_barrier_semaphore()
    for k in range(1, blocks):
        pl.semaphore_signal(
            barrier, inc=1, device_id={"blk": (me + k) % blocks}, device_id_type=MESH
        )
    for k in range(1, copies):
        pl.semaphore_signal(
            barrier, inc=1, device_id={"rep": (rep + k) % copies}, device_id_type=MESH
        )
    loads = [
        pltpu.make_async_copy(src_hbm, slots.at[me], load_sem.at[0]),
        pltpu.make_async_copy(lsw_hbm, lsw, load_sem.at[1]),
        pltpu.make_async_copy(sp_hbm, sp, load_sem.at[2]),
        pltpu.make_async_copy(tgt_hbm, tgt_v, load_sem.at[3]),
        pltpu.make_async_copy(ltw_hbm, ltw, load_sem.at[4]),
        pltpu.make_async_copy(tp_hbm, tp, load_sem.at[5]),
    ]
    for load in loads:
        load.start()
    pl.semaphore_wait(barrier, blocks + copies - 2)

    def slot_copy(place, peer):
        return pltpu.make_async_remote_copy(
            src_ref=src_hbm, dst_ref=slots.at[place],
            send_sem=slot_send.at[peer], recv_sem=slot_recv.at[place],
            device_id={"blk": peer}, device_id_type=MESH,
        )

    def bias_copy(place, peer):
        return pltpu.make_async_remote_copy(
            src_ref=biases.at[me], dst_ref=biases.at[place],
            send_sem=bias_send.at[peer], recv_sem=bias_recv.at[place],
            device_id={"blk": peer}, device_id_type=MESH,
        )

    def row_copy(place, peer):
        return pltpu.make_async_remote_copy(
            src_ref=row_mine.at[peer], dst_ref=row_stats.at[place],
            send_sem=row_send.at[peer], recv_sem=row_recv.at[place],
            device_id={"blk": peer}, device_id_type=MESH,
        )

    def col_copy(place, peer):
        return pltpu.make_async_remote_copy(
            src_ref=col_stats.at[rep], dst_ref=col_stats.at[place],
            send_sem=col_send.at[peer], recv_sem=col_recv.at[place],
            device_id={"rep": peer}, device_id_type=MESH,
        )

    for k in range(1, blocks):
        slot_copy(me, nearest(me, blocks, k)).start()
    for load in loads[:3]:
        load.wait()
    src_bias = lsw[...] + sp[...]
    biases[me] = src_bias - half_square(slots[me])
    for k in range(1, blocks):
        bias_copy(me, nearest(me, blocks, k)).start()
    for load in loads[3:]:
        load.wait()
    tgt_bias = ltw[...] + tp[...]
    tgt_flat[pl.ds(0, bands), :] = tgt_v[...]
    if depth > bands + EXTRA:
        tgt_flat[pl.ds(bands + EXTRA, depth - bands - EXTRA), :] = jnp.zeros(
            (depth - bands - EXTRA, tgt_width), jnp.bfloat16
        )
    tgt_flat[pl.ds(bands, EXTRA), :] = bias_rows(tgt_bias - half_square(tgt_v[...]), 3)
    for at in range(0, tgt_width, TILE):
        tgt_tall[pl.ds(at, TILE), :] = tgt_flat[:, pl.ds(at, TILE)].T
    col_peak[...] = jnp.full_like(col_peak, -jnp.inf)
    col_total[...] = jnp.zeros_like(col_total)

    def turn(k, carry):
        place = nearest(me, blocks, k)

        @pl.when(k > 0)
        def _():
            slot_copy(place, place).wait_recv()
            bias_copy(place, place).wait_recv()

        src = [slots[place], bias_rows(biases[place], 0)]
        if depth > bands + EXTRA:
            src.append(jnp.zeros((depth - bands - EXTRA, width), jnp.bfloat16))
        src = jnp.concatenate(src, axis=0)
        src_tall = src.T
        tiles = range(0, tgt_width, TILE)
        row_peak = None
        for at in tiles:
            block = jnp.dot(tgt_tall[pl.ds(at, TILE), :], src, preferred_element_type=jnp.float32)
            across[pl.ds(at, TILE), :] = block
            peak = jnp.max(grouped(block, WIDE), axis=0)
            row_peak = peak if row_peak is None else jnp.maximum(row_peak, peak)
        col_peaks = []
        for at in tiles:
            block = jnp.dot(
                src_tall, tgt_flat[:, pl.ds(at, TILE)], preferred_element_type=jnp.float32
            )
            down[:, pl.ds(at, TILE)] = block
            peak = jnp.max(grouped(block, WIDE), axis=0)
            col_peaks.append(jnp.max(grouped(peak, SUBLANES), axis=0))
        row_total = None
        for at in tiles:
            block = grouped(across[pl.ds(at, TILE), :], WIDE)
            total = jnp.sum(jnp.exp(block - row_peak[None]), axis=0)
            row_total = total if row_total is None else row_total + total
        top, total = folded(row_peak, row_total)
        stats = jnp.concatenate([top, total], axis=0)

        @pl.when(k > 0)
        def _():
            row_mine[place] = stats
            row_copy(me, place).start()

        @pl.when(k == 0)
        def _():
            row_stats[me] = stats

        for at, peak in zip(tiles, col_peaks):
            here = (slice(None), pl.ds(at, TILE))
            terms = jnp.exp(grouped(down[here], SUBLANES) - peak[None])
            total = jnp.sum(terms.reshape(-1, WIDE, TILE), axis=0)
            total = jnp.sum(grouped(total, SUBLANES), axis=0)
            col_peak[here], col_total[here] = joined(
                (col_peak[here], col_total[here]), (peak, total)
            )
        return carry

    lax.fori_loop(0, blocks, turn, 0)
    top, total = folded(col_peak[...], col_total[...])
    col_stats[rep] = jnp.concatenate([top, total], axis=0)
    for k in range(1, copies):
        col_copy(rep, (rep + k) % copies).start()

    for k in range(1, blocks):
        place = nearest(me, blocks, k)
        row_copy(place, place).wait_recv()
    every = row_stats[...]
    top = jnp.max(every[:, 0, :], axis=0, keepdims=True)
    total = jnp.sum(every[:, 1, :] * jnp.exp(every[:, 0, :] - top), axis=0, keepdims=True)
    src_out[...] = 0.5 * (sp[...] + (src_bias - (top + jnp.log(total))))

    for k in range(1, copies):
        place = (rep + k) % copies
        col_copy(place, place).wait_recv()
    every = col_stats[...]
    top = jnp.max(every[:, 0, :], axis=0, keepdims=True)
    total = jnp.sum(every[:, 1, :] * jnp.exp(every[:, 0, :] - top), axis=0, keepdims=True)
    tgt_out[...] = 0.5 * (tp[...] + (tgt_bias - (top + jnp.log(total))))

    for k in range(1, blocks):
        peer = nearest(me, blocks, k)
        slot_copy(me, peer).wait_send()
        bias_copy(me, peer).wait_send()
        row_copy(me, peer).wait_send()
    for k in range(1, copies):
        col_copy(rep, (rep + k) % copies).wait_send()


def on_device(
    blocks, copies,
    src_spectra, tgt_spectra, log_src_weight, log_tgt_weight, src_potential, tgt_potential,
):
    bands, width = src_spectra.shape
    tgt_width = tgt_spectra.shape[1]
    depth = -(-(bands + EXTRA) // DEPTH) * DEPTH
    one = lambda vector: vector.reshape(1, -1)
    f32, bf16 = jnp.float32, jnp.bfloat16
    dma = pltpu.SemaphoreType.DMA
    elements = blocks * width * tgt_width
    src_updated, tgt_updated = pl.pallas_call(
        functools.partial(kernel, blocks, copies),
        out_shape=(pltpu.VMEM((1, width), f32), pltpu.VMEM((1, tgt_width), f32)),
        in_specs=[pl.BlockSpec(memory_space=pltpu.HBM)] * 6,
        out_specs=(pl.BlockSpec(memory_space=pltpu.VMEM), pl.BlockSpec(memory_space=pltpu.VMEM)),
        scratch_shapes=[
            pltpu.VMEM((blocks, bands, width), bf16),
            pltpu.VMEM((blocks, 1, width), f32),
            pltpu.VMEM((bands, tgt_width), bf16),
            pltpu.VMEM((1, width), f32),
            pltpu.VMEM((1, tgt_width), f32),
            pltpu.VMEM((1, width), f32),
            pltpu.VMEM((1, tgt_width), f32),
            pltpu.VMEM((depth, tgt_width), bf16),
            pltpu.VMEM((tgt_width, depth), bf16),
            pltpu.VMEM((tgt_width, width), f32),
            pltpu.VMEM((width, tgt_width), f32),
            pltpu.VMEM((blocks, 2, width), f32),
            pltpu.VMEM((blocks, 2, width), f32),
            pltpu.VMEM((SUBLANES, tgt_width), f32),
            pltpu.VMEM((SUBLANES, tgt_width), f32),
            pltpu.VMEM((copies, 2, tgt_width), f32),
            dma((6,)),
            dma((blocks,)), dma((blocks,)),
            dma((blocks,)), dma((blocks,)),
            dma((blocks,)), dma((blocks,)),
            dma((copies,)), dma((copies,)),
        ],
        compiler_params=pltpu.CompilerParams(
            collective_id=0, has_side_effects=True, vmem_limit_bytes=32 * 1024 * 1024
        ),
        cost_estimate=pl.CostEstimate(
            flops=4 * elements * bands, bytes_accessed=4 * bands * tgt_width, transcendentals=2 * elements
        ),
        name="sinkhorn",
    )(
        *(
            pltpu.with_memory_space_constraint(array, pltpu.HBM)
            for array in (
                src_spectra, tgt_spectra, one(log_src_weight), one(log_tgt_weight),
                one(src_potential), one(tgt_potential),
            )
        )
    )
    return src_updated.reshape(-1), tgt_updated.reshape(-1)


def solution(mesh):
    placed = (
        P(None, ("pair", "rep", "blk")),
        P(None, ("pair", "blk")),
        P(("pair", "rep", "blk")),
        P(("pair", "blk")),
        P(("pair", "rep", "blk")),
        P(("pair", "blk")),
    )
    return jax.shard_map(
        functools.partial(on_device, mesh.shape["blk"], mesh.shape["rep"]),
        mesh=mesh,
        in_specs=placed,
        out_specs=(P(("pair", "rep", "blk")), P(("pair", "blk"))),
        check_vma=False,
    )
```

```python
import functools

import jax
import jax.numpy as jnp
from jax import lax
from jax.experimental import pallas as pl
from jax.experimental.pallas import tpu as pltpu
from jax.sharding import PartitionSpec as P

MESH = pl.DeviceIdType.MESH
SUBLANES = 8
WIDE = 32
EXTRA = 16
DEPTH = 128
TILE = 256


def nearest(me, count, k):
    short = jnp.minimum(me, count - 1 - me)
    step = (k + 1) // 2
    both = me + jnp.where(k % 2 == 1, step, -step)
    both = jnp.where(me * 2 < count, both, 2 * me - both)
    far = jnp.where(me * 2 < count, k, count - 1 - k)
    return jnp.where(k <= 2 * short, both, far)


def in_three(value):
    high = value.astype(jnp.bfloat16).astype(jnp.float32)
    middle = (value - high).astype(jnp.bfloat16).astype(jnp.float32)
    return high, middle, value - high - middle


def bias_rows(value, first):
    high, middle, low = in_three(value)
    row = lax.broadcasted_iota(jnp.int32, (EXTRA, value.shape[1]), 0)
    out = jnp.where(row < 6, 1.0, 0.0)
    out = jnp.where(row == first, high, out)
    out = jnp.where(row == first + 1, middle, out)
    out = jnp.where(row == first + 2, low, out)
    return out.astype(jnp.bfloat16)


def half_square(block):
    wide = block.astype(jnp.float32)
    return 0.5 * jnp.sum(wide * wide, axis=0, keepdims=True)


def grouped(scores, group):
    rows, width = scores.shape
    return scores.reshape(rows // group, group, width)


def joined(earlier, later):
    peak = jnp.maximum(earlier[0], later[0])
    return peak, earlier[1] * jnp.exp(earlier[0] - peak) + later[1] * jnp.exp(later[0] - peak)


def folded(peak, total):
    top = jnp.max(peak, axis=0, keepdims=True)
    return top, jnp.sum(total * jnp.exp(peak - top), axis=0, keepdims=True)


def kernel(
    blocks, copies,
    src_hbm, tgt_hbm, lsw_hbm, ltw_hbm, sp_hbm, tp_hbm,
    src_out, tgt_out,
    slots, lsw, sp, tgt_v, ltw, tp, tgt_flat, tgt_tall, across, down, row_mine, row_stats, col_peak, col_total,
    col_stats,
    load_sem, slot_send, slot_recv, row_send, row_recv, col_send, col_recv,
):
    me = lax.axis_index("blk")
    rep = lax.axis_index("rep")
    bands, width = src_hbm.shape
    tgt_width = tgt_hbm.shape[1]
    depth = tgt_flat.shape[0]

    barrier = pltpu.get_barrier_semaphore()
    for k in range(1, blocks):
        pl.semaphore_signal(
            barrier, inc=1, device_id={"blk": (me + k) % blocks}, device_id_type=MESH
        )
    for k in range(1, copies):
        pl.semaphore_signal(
            barrier, inc=1, device_id={"rep": (rep + k) % copies}, device_id_type=MESH
        )
    loads = [
        pltpu.make_async_copy(src_hbm, slots.at[me], load_sem.at[0]),
        pltpu.make_async_copy(lsw_hbm, lsw.at[me], load_sem.at[1]),
        pltpu.make_async_copy(sp_hbm, sp.at[me], load_sem.at[2]),
        pltpu.make_async_copy(tgt_hbm, tgt_v, load_sem.at[3]),
        pltpu.make_async_copy(ltw_hbm, ltw, load_sem.at[4]),
        pltpu.make_async_copy(tp_hbm, tp, load_sem.at[5]),
    ]
    for load in loads:
        load.start()
    pl.semaphore_wait(barrier, blocks + copies - 2)

    def source_copies(place, peer):
        return [
            pltpu.make_async_remote_copy(
                src_ref=source, dst_ref=target.at[place],
                send_sem=slot_send.at[at, peer], recv_sem=slot_recv.at[at, place],
                device_id={"blk": peer}, device_id_type=MESH,
            )
            for at, (source, target) in enumerate(((src_hbm, slots), (lsw_hbm, lsw), (sp_hbm, sp)))
        ]

    def row_copy(place, peer):
        return pltpu.make_async_remote_copy(
            src_ref=row_mine.at[peer], dst_ref=row_stats.at[place],
            send_sem=row_send.at[peer], recv_sem=row_recv.at[place],
            device_id={"blk": peer}, device_id_type=MESH,
        )

    def col_copy(place, peer):
        return pltpu.make_async_remote_copy(
            src_ref=col_stats.at[rep], dst_ref=col_stats.at[place],
            send_sem=col_send.at[peer], recv_sem=col_recv.at[place],
            device_id={"rep": peer}, device_id_type=MESH,
        )

    for k in reversed(range(1, blocks)):
        for copy in source_copies(me, nearest(me, blocks, k)):
            copy.start()
    for load in loads:
        load.wait()
    tgt_bias = ltw[...] + tp[...]
    tgt_flat[pl.ds(0, bands), :] = tgt_v[...]
    if depth > bands + EXTRA:
        tgt_flat[pl.ds(bands + EXTRA, depth - bands - EXTRA), :] = jnp.zeros(
            (depth - bands - EXTRA, tgt_width), jnp.bfloat16
        )
    tgt_flat[pl.ds(bands, EXTRA), :] = bias_rows(tgt_bias - half_square(tgt_v[...]), 3)
    for at in range(0, tgt_width, TILE):
        tgt_tall[pl.ds(at, TILE), :] = tgt_flat[:, pl.ds(at, TILE)].T
    col_peak[...] = jnp.full_like(col_peak, -jnp.inf)
    col_total[...] = jnp.zeros_like(col_total)

    def turn(k, carry):
        place = nearest(me, blocks, k)

        @pl.when(k > 0)
        def _():
            for copy in source_copies(place, place):
                copy.wait_recv()

        block = slots[place]
        src = [block, bias_rows(lsw[place] + sp[place] - half_square(block), 0)]
        if depth > bands + EXTRA:
            src.append(jnp.zeros((depth - bands - EXTRA, width), jnp.bfloat16))
        src = jnp.concatenate(src, axis=0)
        src_tall = src.T
        tiles = range(0, tgt_width, TILE)
        row_peak = None
        for at in tiles:
            block = jnp.dot(tgt_tall[pl.ds(at, TILE), :], src, preferred_element_type=jnp.float32)
            across[pl.ds(at, TILE), :] = block
            peak = jnp.max(grouped(block, WIDE), axis=0)
            row_peak = peak if row_peak is None else jnp.maximum(row_peak, peak)
        col_peaks = []
        for at in tiles:
            block = jnp.dot(
                src_tall, tgt_flat[:, pl.ds(at, TILE)], preferred_element_type=jnp.float32
            )
            down[:, pl.ds(at, TILE)] = block
            peak = jnp.max(grouped(block, WIDE), axis=0)
            col_peaks.append(jnp.max(grouped(peak, SUBLANES), axis=0))
        row_total = None
        for at in tiles:
            block = grouped(across[pl.ds(at, TILE), :], WIDE)
            total = jnp.sum(jnp.exp(block - row_peak[None]), axis=0)
            row_total = total if row_total is None else row_total + total
        top, total = folded(row_peak, row_total)
        stats = jnp.concatenate([top, total], axis=0)

        @pl.when(k > 0)
        def _():
            row_mine[place] = stats
            row_copy(me, place).start()

        @pl.when(k == 0)
        def _():
            row_stats[me] = stats

        for at, peak in zip(tiles, col_peaks):
            here = (slice(None), pl.ds(at, TILE))
            terms = jnp.exp(grouped(down[here], SUBLANES) - peak[None])
            total = jnp.sum(terms.reshape(-1, WIDE, TILE), axis=0)
            total = jnp.sum(grouped(total, SUBLANES), axis=0)
            col_peak[here], col_total[here] = joined(
                (col_peak[here], col_total[here]), (peak, total)
            )
        return carry

    lax.fori_loop(0, blocks, turn, 0)
    top, total = folded(col_peak[...], col_total[...])
    col_stats[rep] = jnp.concatenate([top, total], axis=0)
    for k in range(1, copies):
        col_copy(rep, (rep + k) % copies).start()

    for k in range(1, blocks):
        place = nearest(me, blocks, k)
        row_copy(place, place).wait_recv()
    every = row_stats[...]
    top = jnp.max(every[:, 0, :], axis=0, keepdims=True)
    total = jnp.sum(every[:, 1, :] * jnp.exp(every[:, 0, :] - top), axis=0, keepdims=True)
    src_out[...] = 0.5 * (sp[me] + (lsw[me] + sp[me] - (top + jnp.log(total))))

    for k in range(1, copies):
        place = (rep + k) % copies
        col_copy(place, place).wait_recv()
    every = col_stats[...]
    top = jnp.max(every[:, 0, :], axis=0, keepdims=True)
    total = jnp.sum(every[:, 1, :] * jnp.exp(every[:, 0, :] - top), axis=0, keepdims=True)
    tgt_out[...] = 0.5 * (tp[...] + (tgt_bias - (top + jnp.log(total))))

    for k in range(1, blocks):
        peer = nearest(me, blocks, k)
        for copy in source_copies(me, peer):
            copy.wait_send()
        row_copy(me, peer).wait_send()
    for k in range(1, copies):
        col_copy(rep, (rep + k) % copies).wait_send()


def on_device(
    blocks, copies,
    src_spectra, tgt_spectra, log_src_weight, log_tgt_weight, src_potential, tgt_potential,
):
    bands, width = src_spectra.shape
    tgt_width = tgt_spectra.shape[1]
    depth = -(-(bands + EXTRA) // DEPTH) * DEPTH
    one = lambda vector: vector.reshape(1, -1)
    f32, bf16 = jnp.float32, jnp.bfloat16
    dma = pltpu.SemaphoreType.DMA
    elements = blocks * width * tgt_width
    src_updated, tgt_updated = pl.pallas_call(
        functools.partial(kernel, blocks, copies),
        out_shape=(pltpu.VMEM((1, width), f32), pltpu.VMEM((1, tgt_width), f32)),
        in_specs=[pl.BlockSpec(memory_space=pltpu.HBM)] * 6,
        out_specs=(pl.BlockSpec(memory_space=pltpu.VMEM), pl.BlockSpec(memory_space=pltpu.VMEM)),
        scratch_shapes=[
            pltpu.VMEM((blocks, bands, width), bf16),
            pltpu.VMEM((blocks, 1, width), f32),
            pltpu.VMEM((blocks, 1, width), f32),
            pltpu.VMEM((bands, tgt_width), bf16),
            pltpu.VMEM((1, tgt_width), f32),
            pltpu.VMEM((1, tgt_width), f32),
            pltpu.VMEM((depth, tgt_width), bf16),
            pltpu.VMEM((tgt_width, depth), bf16),
            pltpu.VMEM((tgt_width, width), f32),
            pltpu.VMEM((width, tgt_width), f32),
            pltpu.VMEM((blocks, 2, width), f32),
            pltpu.VMEM((blocks, 2, width), f32),
            pltpu.VMEM((SUBLANES, tgt_width), f32),
            pltpu.VMEM((SUBLANES, tgt_width), f32),
            pltpu.VMEM((copies, 2, tgt_width), f32),
            dma((6,)),
            dma((3, blocks)), dma((3, blocks)),
            dma((blocks,)), dma((blocks,)),
            dma((copies,)), dma((copies,)),
        ],
        compiler_params=pltpu.CompilerParams(
            collective_id=0, has_side_effects=True, vmem_limit_bytes=32 * 1024 * 1024
        ),
        cost_estimate=pl.CostEstimate(
            flops=4 * elements * bands, bytes_accessed=4 * bands * tgt_width, transcendentals=2 * elements
        ),
        name="sinkhorn",
    )(
        *(
            pltpu.with_memory_space_constraint(array, pltpu.HBM)
            for array in (
                src_spectra, tgt_spectra, one(log_src_weight), one(log_tgt_weight),
                one(src_potential), one(tgt_potential),
            )
        )
    )
    return src_updated.reshape(-1), tgt_updated.reshape(-1)


def solution(mesh):
    placed = (
        P(None, ("pair", "rep", "blk")),
        P(None, ("pair", "blk")),
        P(("pair", "rep", "blk")),
        P(("pair", "blk")),
        P(("pair", "rep", "blk")),
        P(("pair", "blk")),
    )
    return jax.shard_map(
        functools.partial(on_device, mesh.shape["blk"], mesh.shape["rep"]),
        mesh=mesh,
        in_specs=placed,
        out_specs=(P(("pair", "rep", "blk")), P(("pair", "blk"))),
        check_vma=False,
    )
```

```python
import functools

import jax
import jax.numpy as jnp
from jax import lax
from jax.experimental import pallas as pl
from jax.experimental.pallas import tpu as pltpu
from jax.sharding import PartitionSpec as P

MESH = pl.DeviceIdType.MESH
SUBLANES = 8
WIDE = 32
EXTRA = 16
DEPTH = 128
TILE = 256


def nearest(me, count, k):
    short = jnp.minimum(me, count - 1 - me)
    step = (k + 1) // 2
    both = me + jnp.where(k % 2 == 1, step, -step)
    both = jnp.where(me * 2 < count, both, 2 * me - both)
    far = jnp.where(me * 2 < count, k, count - 1 - k)
    return jnp.where(k <= 2 * short, both, far)


def in_three(value):
    high = value.astype(jnp.bfloat16).astype(jnp.float32)
    middle = (value - high).astype(jnp.bfloat16).astype(jnp.float32)
    return high, middle, value - high - middle


def bias_rows(value, width, first=0):
    row = lax.broadcasted_iota(jnp.int32, (EXTRA, width), 0)
    other = 3 - first
    out = jnp.where((row >= other) & (row < other + 3), 1.0, 0.0)
    if value is not None:
        high, middle, low = in_three(value)
        out = jnp.where(row == first, high, out)
        out = jnp.where(row == first + 1, middle, out)
        out = jnp.where(row == first + 2, low, out)
    return out.astype(jnp.bfloat16)


def half_square(block):
    wide = block.astype(jnp.float32)
    return 0.5 * jnp.sum(wide * wide, axis=0, keepdims=True)


def grouped(scores, group):
    rows, width = scores.shape
    return scores.reshape(rows // group, group, width)


def joined(earlier, later):
    peak = jnp.maximum(earlier[0], later[0])
    return peak, earlier[1] * jnp.exp(earlier[0] - peak) + later[1] * jnp.exp(later[0] - peak)


def folded(peak, total):
    top = jnp.max(peak, axis=0, keepdims=True)
    return top, jnp.sum(total * jnp.exp(peak - top), axis=0, keepdims=True)


def kernel(
    blocks, copies,
    src_hbm, tgt_hbm, lsw_hbm, ltw_hbm, sp_hbm, tp_hbm,
    src_out, tgt_out,
    slots, lsw, sp, tgt_v, ltw, tp, tgt_flat, tgt_tall, across, down, row_mine, row_stats, col_peak, col_total,
    col_stats,
    load_sem, slot_send, slot_recv, row_send, row_recv, col_send, col_recv,
):
    me = lax.axis_index("blk")
    rep = lax.axis_index("rep")
    bands, width = src_hbm.shape
    tgt_width = tgt_hbm.shape[1]
    depth = tgt_flat.shape[0]

    barrier = pltpu.get_barrier_semaphore()
    for k in range(1, blocks):
        pl.semaphore_signal(
            barrier, inc=1, device_id={"blk": (me + k) % blocks}, device_id_type=MESH
        )
    for k in range(1, copies):
        pl.semaphore_signal(
            barrier, inc=1, device_id={"rep": (rep + k) % copies}, device_id_type=MESH
        )
    loads = [
        pltpu.make_async_copy(src_hbm, slots.at[me], load_sem.at[0]),
        pltpu.make_async_copy(lsw_hbm, lsw.at[me], load_sem.at[1]),
        pltpu.make_async_copy(sp_hbm, sp.at[me], load_sem.at[2]),
        pltpu.make_async_copy(tgt_hbm, tgt_v, load_sem.at[3]),
        pltpu.make_async_copy(ltw_hbm, ltw, load_sem.at[4]),
        pltpu.make_async_copy(tp_hbm, tp, load_sem.at[5]),
    ]
    for load in loads:
        load.start()
    pl.semaphore_wait(barrier, blocks + copies - 2)

    def source_copies(place, peer):
        return [
            pltpu.make_async_remote_copy(
                src_ref=source, dst_ref=target.at[place],
                send_sem=slot_send.at[at, peer], recv_sem=slot_recv.at[at, place],
                device_id={"blk": peer}, device_id_type=MESH,
            )
            for at, (source, target) in enumerate(((src_hbm, slots), (lsw_hbm, lsw), (sp_hbm, sp)))
        ]

    def row_copy(place, peer):
        return pltpu.make_async_remote_copy(
            src_ref=row_mine.at[peer], dst_ref=row_stats.at[place],
            send_sem=row_send.at[peer], recv_sem=row_recv.at[place],
            device_id={"blk": peer}, device_id_type=MESH,
        )

    def col_copy(place, peer):
        return pltpu.make_async_remote_copy(
            src_ref=col_stats.at[rep], dst_ref=col_stats.at[place],
            send_sem=col_send.at[peer], recv_sem=col_recv.at[place],
            device_id={"rep": peer}, device_id_type=MESH,
        )

    for k in reversed(range(1, blocks)):
        for copy in source_copies(me, nearest(me, blocks, k)):
            copy.start()
    for load in loads:
        load.wait()
    tgt_bias = ltw[...] + tp[...]
    tgt_flat[pl.ds(0, bands), :] = tgt_v[...]
    if depth > bands + EXTRA:
        tgt_flat[pl.ds(bands + EXTRA, depth - bands - EXTRA), :] = jnp.zeros(
            (depth - bands - EXTRA, tgt_width), jnp.bfloat16
        )
    tgt_flat[pl.ds(bands, EXTRA), :] = bias_rows(
        tgt_bias - half_square(tgt_v[...]), tgt_width, 3
    )
    for at in range(0, tgt_width, TILE):
        tgt_tall[pl.ds(at, TILE), :] = tgt_flat[:, pl.ds(at, TILE)].T
    col_peak[...] = jnp.full_like(col_peak, -jnp.inf)
    col_total[...] = jnp.zeros_like(col_total)

    src_square = half_square(slots[me])

    def deepened(block, extra):
        pieces = [block, extra]
        if depth > bands + EXTRA:
            pieces.append(jnp.zeros((depth - bands - EXTRA, width), jnp.bfloat16))
        return jnp.concatenate(pieces, axis=0)

    def turn(k, carry):
        place = nearest(me, blocks, k)

        @pl.when(k > 0)
        def _():
            for copy in source_copies(place, place):
                copy.wait_recv()

        own = slots[place]
        src = deepened(own, bias_rows(None, width))
        src_tall = deepened(own, bias_rows(lsw[place] + sp[place] - half_square(own), width)).T
        tiles = range(0, tgt_width, TILE)
        row_peak = None
        for at in tiles:
            block = jnp.dot(tgt_tall[pl.ds(at, TILE), :], src, preferred_element_type=jnp.float32)
            across[pl.ds(at, TILE), :] = block
            peak = jnp.max(grouped(block, WIDE), axis=0)
            row_peak = peak if row_peak is None else jnp.maximum(row_peak, peak)
        col_peaks = []
        for at in tiles:
            block = jnp.dot(
                src_tall, tgt_flat[:, pl.ds(at, TILE)], preferred_element_type=jnp.float32
            )
            down[:, pl.ds(at, TILE)] = block
            peak = jnp.max(grouped(block, WIDE), axis=0)
            col_peaks.append(jnp.max(grouped(peak, SUBLANES), axis=0))
        row_total = None
        for at in tiles:
            block = grouped(across[pl.ds(at, TILE), :], WIDE)
            total = jnp.sum(jnp.exp(block - row_peak[None]), axis=0)
            row_total = total if row_total is None else row_total + total
        top, total = folded(row_peak, row_total)
        stats = jnp.concatenate([top, total], axis=0)

        @pl.when(k > 0)
        def _():
            row_mine[place] = stats
            row_copy(me, place).start()

        @pl.when(k == 0)
        def _():
            row_stats[me] = stats

        for at, peak in zip(tiles, col_peaks):
            here = (slice(None), pl.ds(at, TILE))
            terms = jnp.exp(grouped(down[here], SUBLANES) - peak[None])
            total = jnp.sum(terms.reshape(-1, WIDE, TILE), axis=0)
            total = jnp.sum(grouped(total, SUBLANES), axis=0)
            col_peak[here], col_total[here] = joined(
                (col_peak[here], col_total[here]), (peak, total)
            )
        return carry

    lax.fori_loop(0, blocks, turn, 0)
    top, total = folded(col_peak[...], col_total[...])
    col_stats[rep] = jnp.concatenate([top, total], axis=0)
    for k in range(1, copies):
        col_copy(rep, (rep + k) % copies).start()

    for k in range(1, blocks):
        place = nearest(me, blocks, k)
        row_copy(place, place).wait_recv()
    every = row_stats[...]
    top = jnp.max(every[:, 0, :], axis=0, keepdims=True)
    total = jnp.sum(every[:, 1, :] * jnp.exp(every[:, 0, :] - top), axis=0, keepdims=True)
    src_out[...] = 0.5 * (sp[me] + (src_square - (top + jnp.log(total))))

    for k in range(1, copies):
        place = (rep + k) % copies
        col_copy(place, place).wait_recv()
    every = col_stats[...]
    top = jnp.max(every[:, 0, :], axis=0, keepdims=True)
    total = jnp.sum(every[:, 1, :] * jnp.exp(every[:, 0, :] - top), axis=0, keepdims=True)
    tgt_out[...] = 0.5 * (tp[...] + (tgt_bias - (top + jnp.log(total))))

    for k in range(1, blocks):
        peer = nearest(me, blocks, k)
        for copy in source_copies(me, peer):
            copy.wait_send()
        row_copy(me, peer).wait_send()
    for k in range(1, copies):
        col_copy(rep, (rep + k) % copies).wait_send()


def on_device(
    blocks, copies,
    src_spectra, tgt_spectra, log_src_weight, log_tgt_weight, src_potential, tgt_potential,
):
    bands, width = src_spectra.shape
    tgt_width = tgt_spectra.shape[1]
    depth = -(-(bands + EXTRA) // DEPTH) * DEPTH
    one = lambda vector: vector.reshape(1, -1)
    f32, bf16 = jnp.float32, jnp.bfloat16
    dma = pltpu.SemaphoreType.DMA
    elements = blocks * width * tgt_width
    src_updated, tgt_updated = pl.pallas_call(
        functools.partial(kernel, blocks, copies),
        out_shape=(pltpu.VMEM((1, width), f32), pltpu.VMEM((1, tgt_width), f32)),
        in_specs=[pl.BlockSpec(memory_space=pltpu.HBM)] * 6,
        out_specs=(pl.BlockSpec(memory_space=pltpu.VMEM), pl.BlockSpec(memory_space=pltpu.VMEM)),
        scratch_shapes=[
            pltpu.VMEM((blocks, bands, width), bf16),
            pltpu.VMEM((blocks, 1, width), f32),
            pltpu.VMEM((blocks, 1, width), f32),
            pltpu.VMEM((bands, tgt_width), bf16),
            pltpu.VMEM((1, tgt_width), f32),
            pltpu.VMEM((1, tgt_width), f32),
            pltpu.VMEM((depth, tgt_width), bf16),
            pltpu.VMEM((tgt_width, depth), bf16),
            pltpu.VMEM((tgt_width, width), f32),
            pltpu.VMEM((width, tgt_width), f32),
            pltpu.VMEM((blocks, 2, width), f32),
            pltpu.VMEM((blocks, 2, width), f32),
            pltpu.VMEM((SUBLANES, tgt_width), f32),
            pltpu.VMEM((SUBLANES, tgt_width), f32),
            pltpu.VMEM((copies, 2, tgt_width), f32),
            dma((6,)),
            dma((3, blocks)), dma((3, blocks)),
            dma((blocks,)), dma((blocks,)),
            dma((copies,)), dma((copies,)),
        ],
        compiler_params=pltpu.CompilerParams(
            collective_id=0, has_side_effects=True, vmem_limit_bytes=32 * 1024 * 1024
        ),
        cost_estimate=pl.CostEstimate(
            flops=4 * elements * bands, bytes_accessed=4 * bands * tgt_width, transcendentals=2 * elements
        ),
        name="sinkhorn",
    )(
        *(
            pltpu.with_memory_space_constraint(array, pltpu.HBM)
            for array in (
                src_spectra, tgt_spectra, one(log_src_weight), one(log_tgt_weight),
                one(src_potential), one(tgt_potential),
            )
        )
    )
    return src_updated.reshape(-1), tgt_updated.reshape(-1)


def solution(mesh):
    placed = (
        P(None, ("pair", "rep", "blk")),
        P(None, ("pair", "blk")),
        P(("pair", "rep", "blk")),
        P(("pair", "blk")),
        P(("pair", "rep", "blk")),
        P(("pair", "blk")),
    )
    return jax.shard_map(
        functools.partial(on_device, mesh.shape["blk"], mesh.shape["rep"]),
        mesh=mesh,
        in_specs=placed,
        out_specs=(P(("pair", "rep", "blk")), P(("pair", "blk"))),
        check_vma=False,
    )
```

```python
import functools

import jax
import jax.numpy as jnp
from jax import lax
from jax.experimental import pallas as pl
from jax.experimental.pallas import tpu as pltpu
from jax.sharding import PartitionSpec as P

MESH = pl.DeviceIdType.MESH
SUBLANES = 8
WIDE = 32
EXTRA = 16
DEPTH = 128
TILE = 256
LOG2_E = 1.4426950408889634


def nearest(me, count, k):
    short = jnp.minimum(me, count - 1 - me)
    step = (k + 1) // 2
    both = me + jnp.where(k % 2 == 1, step, -step)
    both = jnp.where(me * 2 < count, both, 2 * me - both)
    far = jnp.where(me * 2 < count, k, count - 1 - k)
    return jnp.where(k <= 2 * short, both, far)


def power(value):
    return jnp.exp2(value * LOG2_E)


def in_three(value):
    high = value.astype(jnp.bfloat16).astype(jnp.float32)
    middle = (value - high).astype(jnp.bfloat16).astype(jnp.float32)
    return high, middle, value - high - middle


def bias_rows(value, width, first=0):
    row = lax.broadcasted_iota(jnp.int32, (EXTRA, width), 0)
    other = 3 - first
    out = jnp.where((row >= other) & (row < other + 3), 1.0, 0.0)
    if value is not None:
        high, middle, low = in_three(value)
        out = jnp.where(row == first, high, out)
        out = jnp.where(row == first + 1, middle, out)
        out = jnp.where(row == first + 2, low, out)
    return out.astype(jnp.bfloat16)


def half_square(block):
    wide = block.astype(jnp.float32)
    return 0.5 * jnp.sum(wide * wide, axis=0, keepdims=True)


def grouped(scores, group):
    rows, width = scores.shape
    return scores.reshape(rows // group, group, width)


def joined(earlier, later):
    peak = jnp.maximum(earlier[0], later[0])
    return peak, earlier[1] * power(earlier[0] - peak) + later[1] * power(later[0] - peak)


def folded(peak, total):
    top = jnp.max(peak, axis=0, keepdims=True)
    return top, jnp.sum(total * power(peak - top), axis=0, keepdims=True)


def kernel(
    blocks, copies,
    src_hbm, tgt_hbm, lsw_hbm, ltw_hbm, sp_hbm, tp_hbm,
    src_out, tgt_out,
    slots, lsw, sp, tgt_v, ltw, tp, tgt_flat, tgt_tall, across, down, row_mine, row_stats, col_peak, col_total,
    col_stats,
    load_sem, slot_send, slot_recv, row_send, row_recv, col_send, col_recv,
):
    me = lax.axis_index("blk")
    rep = lax.axis_index("rep")
    bands, width = src_hbm.shape
    tgt_width = tgt_hbm.shape[1]
    depth = tgt_flat.shape[0]

    barrier = pltpu.get_barrier_semaphore()
    for k in range(1, blocks):
        pl.semaphore_signal(
            barrier, inc=1, device_id={"blk": (me + k) % blocks}, device_id_type=MESH
        )
    for k in range(1, copies):
        pl.semaphore_signal(
            barrier, inc=1, device_id={"rep": (rep + k) % copies}, device_id_type=MESH
        )
    loads = [
        pltpu.make_async_copy(src_hbm, slots.at[me], load_sem.at[0]),
        pltpu.make_async_copy(lsw_hbm, lsw.at[me], load_sem.at[1]),
        pltpu.make_async_copy(sp_hbm, sp.at[me], load_sem.at[2]),
        pltpu.make_async_copy(tgt_hbm, tgt_v, load_sem.at[3]),
        pltpu.make_async_copy(ltw_hbm, ltw, load_sem.at[4]),
        pltpu.make_async_copy(tp_hbm, tp, load_sem.at[5]),
    ]
    for load in loads:
        load.start()
    pl.semaphore_wait(barrier, blocks + copies - 2)

    def source_copies(place, peer):
        return [
            pltpu.make_async_remote_copy(
                src_ref=source, dst_ref=target.at[place],
                send_sem=slot_send.at[at, peer], recv_sem=slot_recv.at[at, place],
                device_id={"blk": peer}, device_id_type=MESH,
            )
            for at, (source, target) in enumerate(((src_hbm, slots), (lsw_hbm, lsw), (sp_hbm, sp)))
        ]

    def row_copy(place, peer):
        return pltpu.make_async_remote_copy(
            src_ref=row_mine.at[peer], dst_ref=row_stats.at[place],
            send_sem=row_send.at[peer], recv_sem=row_recv.at[place],
            device_id={"blk": peer}, device_id_type=MESH,
        )

    def col_copy(place, peer):
        return pltpu.make_async_remote_copy(
            src_ref=col_stats.at[rep], dst_ref=col_stats.at[place],
            send_sem=col_send.at[peer], recv_sem=col_recv.at[place],
            device_id={"rep": peer}, device_id_type=MESH,
        )

    for k in reversed(range(1, blocks)):
        for copy in source_copies(me, nearest(me, blocks, k)):
            copy.start()
    for load in loads:
        load.wait()
    tgt_bias = ltw[...] + tp[...]
    tgt_flat[pl.ds(0, bands), :] = tgt_v[...]
    if depth > bands + EXTRA:
        tgt_flat[pl.ds(bands + EXTRA, depth - bands - EXTRA), :] = jnp.zeros(
            (depth - bands - EXTRA, tgt_width), jnp.bfloat16
        )
    tgt_flat[pl.ds(bands, EXTRA), :] = bias_rows(
        tgt_bias - half_square(tgt_v[...]), tgt_width, 3
    )
    for at in range(0, tgt_width, TILE):
        tgt_tall[pl.ds(at, TILE), :] = tgt_flat[:, pl.ds(at, TILE)].T
    col_peak[...] = jnp.full_like(col_peak, -jnp.inf)
    col_total[...] = jnp.zeros_like(col_total)

    src_square = half_square(slots[me])

    def deepened(block, extra):
        pieces = [block, extra]
        if depth > bands + EXTRA:
            pieces.append(jnp.zeros((depth - bands - EXTRA, width), jnp.bfloat16))
        return jnp.concatenate(pieces, axis=0)

    def turn(k, carry):
        place = nearest(me, blocks, k)

        @pl.when(k > 0)
        def _():
            for copy in source_copies(place, place):
                copy.wait_recv()

        own = slots[place]
        src = deepened(own, bias_rows(None, width))
        src_tall = deepened(own, bias_rows(lsw[place] + sp[place] - half_square(own), width)).T
        tiles = range(0, tgt_width, TILE)
        row_peak = None
        for at in tiles:
            block = jnp.dot(tgt_tall[pl.ds(at, TILE), :], src, preferred_element_type=jnp.float32)
            across[pl.ds(at, TILE), :] = block
            peak = jnp.max(grouped(block, WIDE), axis=0)
            row_peak = peak if row_peak is None else jnp.maximum(row_peak, peak)
        col_peaks = []
        for at in tiles:
            block = jnp.dot(
                src_tall, tgt_flat[:, pl.ds(at, TILE)], preferred_element_type=jnp.float32
            )
            down[:, pl.ds(at, TILE)] = block
            peak = jnp.max(grouped(block, WIDE), axis=0)
            col_peaks.append(jnp.max(grouped(peak, SUBLANES), axis=0))
        row_total = None
        for at in tiles:
            block = grouped(across[pl.ds(at, TILE), :], WIDE)
            total = jnp.sum(power(block - row_peak[None]), axis=0)
            row_total = total if row_total is None else row_total + total
        top, total = folded(row_peak, row_total)
        stats = jnp.concatenate([top, total], axis=0)

        @pl.when(k > 0)
        def _():
            row_mine[place] = stats
            row_copy(me, place).start()

        @pl.when(k == 0)
        def _():
            row_stats[me] = stats

        for at, peak in zip(tiles, col_peaks):
            here = (slice(None), pl.ds(at, TILE))
            terms = power(grouped(down[here], SUBLANES) - peak[None])
            total = jnp.sum(terms.reshape(-1, WIDE, TILE), axis=0)
            total = jnp.sum(grouped(total, SUBLANES), axis=0)
            col_peak[here], col_total[here] = joined(
                (col_peak[here], col_total[here]), (peak, total)
            )
        return carry

    lax.fori_loop(0, blocks, turn, 0)
    top, total = folded(col_peak[...], col_total[...])
    col_stats[rep] = jnp.concatenate([top, total], axis=0)
    for k in range(1, copies):
        col_copy(rep, (rep + k) % copies).start()

    for k in range(1, blocks):
        place = nearest(me, blocks, k)
        row_copy(place, place).wait_recv()
    every = row_stats[...]
    top = jnp.max(every[:, 0, :], axis=0, keepdims=True)
    total = jnp.sum(every[:, 1, :] * power(every[:, 0, :] - top), axis=0, keepdims=True)
    src_out[...] = 0.5 * (sp[me] + (src_square - (top + jnp.log(total))))

    for k in range(1, copies):
        place = (rep + k) % copies
        col_copy(place, place).wait_recv()
    every = col_stats[...]
    top = jnp.max(every[:, 0, :], axis=0, keepdims=True)
    total = jnp.sum(every[:, 1, :] * power(every[:, 0, :] - top), axis=0, keepdims=True)
    tgt_out[...] = 0.5 * (tp[...] + (tgt_bias - (top + jnp.log(total))))

    for k in range(1, blocks):
        peer = nearest(me, blocks, k)
        for copy in source_copies(me, peer):
            copy.wait_send()
        row_copy(me, peer).wait_send()
    for k in range(1, copies):
        col_copy(rep, (rep + k) % copies).wait_send()


def on_device(
    blocks, copies,
    src_spectra, tgt_spectra, log_src_weight, log_tgt_weight, src_potential, tgt_potential,
):
    bands, width = src_spectra.shape
    tgt_width = tgt_spectra.shape[1]
    depth = -(-(bands + EXTRA) // DEPTH) * DEPTH
    one = lambda vector: vector.reshape(1, -1)
    f32, bf16 = jnp.float32, jnp.bfloat16
    dma = pltpu.SemaphoreType.DMA
    elements = blocks * width * tgt_width
    src_updated, tgt_updated = pl.pallas_call(
        functools.partial(kernel, blocks, copies),
        out_shape=(pltpu.VMEM((1, width), f32), pltpu.VMEM((1, tgt_width), f32)),
        in_specs=[pl.BlockSpec(memory_space=pltpu.HBM)] * 6,
        out_specs=(pl.BlockSpec(memory_space=pltpu.VMEM), pl.BlockSpec(memory_space=pltpu.VMEM)),
        scratch_shapes=[
            pltpu.VMEM((blocks, bands, width), bf16),
            pltpu.VMEM((blocks, 1, width), f32),
            pltpu.VMEM((blocks, 1, width), f32),
            pltpu.VMEM((bands, tgt_width), bf16),
            pltpu.VMEM((1, tgt_width), f32),
            pltpu.VMEM((1, tgt_width), f32),
            pltpu.VMEM((depth, tgt_width), bf16),
            pltpu.VMEM((tgt_width, depth), bf16),
            pltpu.VMEM((tgt_width, width), f32),
            pltpu.VMEM((width, tgt_width), f32),
            pltpu.VMEM((blocks, 2, width), f32),
            pltpu.VMEM((blocks, 2, width), f32),
            pltpu.VMEM((SUBLANES, tgt_width), f32),
            pltpu.VMEM((SUBLANES, tgt_width), f32),
            pltpu.VMEM((copies, 2, tgt_width), f32),
            dma((6,)),
            dma((3, blocks)), dma((3, blocks)),
            dma((blocks,)), dma((blocks,)),
            dma((copies,)), dma((copies,)),
        ],
        compiler_params=pltpu.CompilerParams(
            collective_id=0, has_side_effects=True, vmem_limit_bytes=32 * 1024 * 1024
        ),
        cost_estimate=pl.CostEstimate(
            flops=4 * elements * bands, bytes_accessed=4 * bands * tgt_width, transcendentals=2 * elements
        ),
        name="sinkhorn",
    )(
        *(
            pltpu.with_memory_space_constraint(array, pltpu.HBM)
            for array in (
                src_spectra, tgt_spectra, one(log_src_weight), one(log_tgt_weight),
                one(src_potential), one(tgt_potential),
            )
        )
    )
    return src_updated.reshape(-1), tgt_updated.reshape(-1)


def solution(mesh):
    placed = (
        P(None, ("pair", "rep", "blk")),
        P(None, ("pair", "blk")),
        P(("pair", "rep", "blk")),
        P(("pair", "blk")),
        P(("pair", "rep", "blk")),
        P(("pair", "blk")),
    )
    return jax.shard_map(
        functools.partial(on_device, mesh.shape["blk"], mesh.shape["rep"]),
        mesh=mesh,
        in_specs=placed,
        out_specs=(P(("pair", "rep", "blk")), P(("pair", "blk"))),
        check_vma=False,
    )
```
